512 devices in a mesh: row: 64 (over z_lo, x, y), col: 8 (over z_hi, core).
Axes of the slice: x: 4, y: 4, z: 16 (z_hi: 4, z_lo: 4; z = z_hi * 4 + z_lo), core: 2. Of those that a mesh axis runs over, the one named last changes fastest.
Arguments:
- latent: bfloat16 [64, 32, 64, 640], P('row', None, 'col')
- stale_rim: bfloat16 [64, 32, 64, 640], P('row', None, 'col'), may hold values from -4 to 4
- stale_kv: bfloat16 [2, 64, 32, 64, 640], P(None, 'row', None, 'col'), may hold values from -96 to 96
- norm_gain: float32 [640], replicated, may hold values from 0.1 to 1.9
- norm_shift: float32 [640], replicated, may hold values from -2 to 2
- conv_weight: bfloat16 [9, 640, 640], P(None, 'row'), may hold values from -0.078125 to 0.078125
- conv_bias: float32 [640], replicated, may hold values from -2.5 to 2.5
- attn_gain: float32 [640], replicated, may hold values from 0.1 to 1.9
- qkv_weight: bfloat16 [640, 1920], P('row'), may hold values from -0.25 to 0.25
Outputs:
- block_out: bfloat16 [64, 32, 64, 640], P('row', None, 'col')
- attended: bfloat16 [64, 32, 64, 640], P('row', None, 'col')
- fresh_kv: bfloat16 [2, 64, 32, 64, 640], P(None, 'row', None, 'col')
The draws below stay inside these ranges and needn't reach their ends.
All inputs are finite; a program needn't handle non-finite values.
Results may differ from the reference program's by a relative error of at most 0.025.
Values may be sent and summed in bfloat16 or wider, within the bound.
A program may use at most 128 MiB of HBM per device.

```python
import jax
import jax.numpy as jnp
from jax import lax

H = 32
PC = 8
HEADS = 10
HEAD_DIM = 64
GROUPS = 16
C = 640
W = 64
IMAGES = 64
N_COL = 8


def draw_latent(key, part):
    key = jax.random.fold_in(key, 1)
    key_base, key_offset = jax.random.split(key)
    columns = jnp.arange(W, dtype=jnp.float32) / W
    base = jax.random.normal(key_base, (IMAGES, H, W, C), jnp.float32)
    col_scale = 1.0 + 2.0 * columns
    offset = 0.3 * jax.random.normal(key_offset, (C,), jnp.float32)
    return (base * col_scale[None, None, :, None] + offset).astype(jnp.bfloat16)


def draw_stale_kv(key, part):
    key = jax.random.fold_in(key, 2)
    key_base = jax.random.fold_in(key, 0)
    result = jnp.clip(jax.random.normal(key_base, (2, IMAGES, H, W, C), jnp.float32), -6.0, 6.0)
    return result.astype(jnp.bfloat16)


def block_scale(key, extent, cuts, low, top_value):
    level, own = 1.0, jax.random.fold_in(key, 6)
    for position, blocks in cuts:
        heights = jnp.exp(jax.random.uniform(jax.random.fold_in(own, position), (blocks,), jnp.float32, low / len(cuts), top_value / len(cuts)))
        level = level * jnp.repeat(heights, extent[position] // blocks).reshape([-1 if axis == position else 1 for axis in range(len(extent))])
    return level


def normal_values(key, dims, width, limit, shards=(), kind=jnp.bfloat16):
    level = block_scale(key, dims, shards, -0.22, 0.18) if shards else 1.0
    values = jax.random.normal(key, dims, jnp.float32) * width * level
    return jnp.minimum(jnp.maximum(values, -limit), limit).astype(kind)


def setup_inputs(seed: int = 0) -> dict:
    seeds = jax.random.split(jax.random.key(seed), 10)
    latent = draw_latent(jax.random.fold_in(seeds[9], 71), 0)
    stale_rim = normal_values(seeds[1], (IMAGES, H, W, C), 0.6, 4.0, ((0, 64), (2, 8)))
    stale_kv = draw_stale_kv(jax.random.fold_in(seeds[9], 71), 0)
    norm_gain = jnp.clip(1.0 + 0.18 * jax.random.normal(seeds[3], (C,), jnp.float32), 0.1, 1.9)
    norm_shift = normal_values(seeds[4], (C,), 0.4, 2.0, (), jnp.float32)
    conv_weight = normal_values(seeds[5], (9, C, C), (9 * C) ** -0.5, 0.078125, ((1, 64),))
    conv_bias = normal_values(seeds[6], (C,), 0.5, 2.5, (), jnp.float32)
    attn_gain = jnp.clip(1.0 + 0.18 * jax.random.normal(seeds[7], (C,), jnp.float32), 0.1, 1.9)
    qkv_weight = normal_values(seeds[8], (C, 3 * C), C ** -0.5, 0.25, ((0, 64),))
    return {"latent": latent, "stale_rim": stale_rim, "stale_kv": stale_kv, "norm_gain": norm_gain, "norm_shift": norm_shift, "conv_weight": conv_weight, "conv_bias": conv_bias, "attn_gain": attn_gain, "qkv_weight": qkv_weight}


EPS = 1e-05

def group_silu(latent, norm_gain, norm_shift):
    images = latent.shape[0]
    grouped = latent.reshape(images, H * W, GROUPS, C // GROUPS).astype(jnp.float32)
    count = H * W * (C // GROUPS)
    first = lax.optimization_barrier(jnp.sum(grouped, axis=(1, 3)))
    second = lax.optimization_barrier(jnp.sum(grouped * grouped, axis=(1, 3)))
    average = first / count
    spread = second / count - average * average
    normed = (grouped - average[:, None, :, None]) * lax.rsqrt(spread + EPS)[:, None, :, None]
    normed = normed.reshape(images, H, W, C) * norm_gain + norm_shift
    return jax.nn.silu(normed).astype(jnp.bfloat16)

def by_device(array):
    return array.reshape(IMAGES, H, N_COL, PC, C).transpose(0, 2, 1, 3, 4).reshape(IMAGES * N_COL, H * PC, C)

def reference(latent, stale_rim, stale_kv, norm_gain, norm_shift, conv_weight, conv_bias, attn_gain, qkv_weight):
    cells = IMAGES * H * W
    tokens = latent.reshape(cells, C).astype(jnp.float32)
    fresh = group_silu(latent, norm_gain, norm_shift)
    pad_spec = ((0, 0), (1, 1), (1, 1), (0, 0))
    padded_fresh = jnp.pad(fresh, pad_spec)
    padded_stale = jnp.pad(stale_rim, pad_spec)
    col_ids = jnp.arange(W, dtype=jnp.int32)
    summed = jnp.zeros((cells, C), jnp.float32)
    for tap_row in range(3):
        for tap_col in range(3):
            same_strip = (col_ids + (tap_col - 1)) // PC == col_ids // PC
            window = jnp.where(same_strip[None, None, :, None], padded_fresh[:, tap_row:tap_row + H, tap_col:tap_col + W], padded_stale[:, tap_row:tap_row + H, tap_col:tap_col + W])
            summed = summed + jnp.dot(window.reshape(cells, C), conv_weight[tap_row * 3 + tap_col], preferred_element_type=jnp.float32)
    block = (tokens + summed + conv_bias).astype(jnp.bfloat16)
    rows_float = block.astype(jnp.float32)
    row_mean = lax.optimization_barrier(jnp.mean(rows_float, axis=1, keepdims=True))
    centered = rows_float - row_mean
    row_var = lax.optimization_barrier(jnp.mean(centered * centered, axis=1, keepdims=True))
    normed = (centered * lax.rsqrt(row_var + EPS) * attn_gain).astype(jnp.bfloat16)
    projected = jnp.dot(normed, qkv_weight, preferred_element_type=jnp.float32).astype(jnp.bfloat16)
    queries = projected[:, :C]
    keys = projected[:, C:2 * C]
    values = projected[:, 2 * C:]
    fresh_kv = jnp.stack([keys, values]).reshape(2, IMAGES, H, W, C)
    devices_all = IMAGES * N_COL
    strip = H * PC
    query_dev = by_device(queries).astype(jnp.float32).reshape(devices_all, strip, HEADS, HEAD_DIM)
    key_dev = by_device(keys).astype(jnp.float32).reshape(devices_all, strip, HEADS, HEAD_DIM)
    value_dev = by_device(values).astype(jnp.float32).reshape(devices_all, strip, HEADS, HEAD_DIM)
    old_keys = stale_kv[0].astype(jnp.float32).reshape(IMAGES, H * W, HEADS, HEAD_DIM)
    old_values = stale_kv[1].astype(jnp.float32).reshape(IMAGES, H * W, HEADS, HEAD_DIM)
    owner = jnp.arange(H * W, dtype=jnp.int32) % W // PC
    factor = HEAD_DIM ** (-0.5)

    def one_device(index):
        image = index // N_COL
        strip_index = index % N_COL
        query = query_dev[index]
        image_keys = old_keys[image]
        image_values = old_values[image]
        score_old = jnp.einsum('qhd,khd->hqk', query, image_keys) * factor
        score_old = jnp.where((owner == strip_index)[None, None, :], -jnp.inf, score_old)
        score_new = jnp.einsum('qhd,khd->hqk', query, key_dev[index]) * factor
        top = jnp.maximum(lax.optimization_barrier(jnp.max(score_old, axis=2)), lax.optimization_barrier(jnp.max(score_new, axis=2)))
        weight_old = jnp.exp(score_old - top[:, :, None])
        weight_new = jnp.exp(score_new - top[:, :, None])
        denom = lax.optimization_barrier(jnp.sum(weight_old, axis=2)) + lax.optimization_barrier(jnp.sum(weight_new, axis=2))
        rounded_old = weight_old.astype(jnp.bfloat16).astype(jnp.float32)
        rounded_new = weight_new.astype(jnp.bfloat16).astype(jnp.float32)
        numer = jnp.einsum('hqk,khd->hqd', rounded_old, image_values) + jnp.einsum('hqk,khd->hqd', rounded_new, value_dev[index])
        result = numer / denom[:, :, None]
        return result.transpose(1, 0, 2).reshape(strip, C).astype(jnp.bfloat16)
    outputs = lax.map(one_device, jnp.arange(devices_all, dtype=jnp.int32))
    attended = outputs.reshape(IMAGES, N_COL, H, PC, C).transpose(0, 2, 1, 3, 4).reshape(IMAGES, H, W, C)
    return (block.reshape(IMAGES, H, W, C), attended, fresh_kv)
```

```python
import jax
import jax.numpy as jnp
from jax import lax
from jax.experimental import pallas as pl
from jax.experimental.pallas import tpu as pltpu
from jax.sharding import PartitionSpec as P

HEADS = 10
HEAD_DIM = 64
GROUPS = 16
C = 640
ROWS = 32
COLS = 8
T = ROWS * COLS
STRIPS = 8
SHARD = 10
SHARDS = 64
PAIRS = 5
EPS = 1e-05
LOG2E = 1.4426950408889634
MESH = pl.DeviceIdType.MESH
F32 = jnp.float32
BF16 = jnp.bfloat16


def iota(shape, dim):
    return lax.broadcasted_iota(jnp.int32, shape, dim)


def kernel(
    lat_ref, rim_ref, kv_ref, gain_ref, shift_ref, w_ref, bias_ref, again_ref,
    block_ref, att_ref, fkv_ref,
    wg, kvg, stats, edges, halo, packed, conv_acc, wq, q2, top, total, accum,
    sems, arr_wz, arr_wa, arr_wb, arr_ws, arr_st, arr_h, arr_k, arr_kf, arr_ks,
):
    row, col = lax.axis_index("row"), lax.axis_index("col")
    zl, xy = lax.div(row, 16), lax.rem(row, 16)
    x, y = lax.div(xy, 4), lax.rem(xy, 4)
    zh, core = lax.div(col, 2), lax.rem(col, 2)
    a, b = x + core * (y - x), y + core * (x - y)
    sa, sb = 4 - 3 * core, 1 + 3 * core

    def ring(value, size):
        return lax.rem(value + size, size)

    def at_a(step):
        return (zl * 16 + ring(a + step, 4) * sa + b * sb, col)

    def at_b(step):
        return (zl * 16 + a * sa + ring(b + step, 4) * sb, col)

    def at_z(step):
        z = ring(zh * 4 + zl + step, 16)
        return (lax.rem(z, 4) * 16 + xy, lax.div(z, 4) * 2 + core)

    def at_zh(step):
        return (row, ring(zh + step, 4) * 2 + core)

    def at_col(step):
        return (row, ring(col + step, 8))

    sibling = (row, col + 1 - 2 * core)
    cross = at_col(2 * core - 1)

    barrier = pltpu.get_barrier_semaphore()
    partners = [at_a(1), at_a(-1), at_b(1), at_b(-1), at_z(1), at_z(-1)]
    partners += [at_zh(1), at_zh(-1), at_zh(2), sibling, cross]
    for partner in partners:
        pl.semaphore_signal(barrier, inc=1, device_id=partner, device_id_type=MESH)

    sent = []

    def copy(src, dst, arrived, device):
        return pltpu.make_async_remote_copy(
            src_ref=src, dst_ref=dst, send_sem=sems.at[len(sent)], recv_sem=arrived,
            device_id=device, device_id_type=MESH,
        )

    def send(src, dst, arrived, device):
        started = copy(src, dst, arrived, device)
        started.start()
        sent.append(started)

    def landed(dst, arrived):
        pltpu.make_async_remote_copy(
            src_ref=dst, dst_ref=dst, send_sem=sems.at[0], recv_sem=arrived,
            device_id=sibling, device_id_type=MESH,
        ).wait_recv()

    half = pl.ds(2 * core, 2)

    wg[half, pl.ds(row, 1)] = w_ref[half][:, None]
    rim = rim_ref[...].astype(F32)
    edges[0] = rim[:, 0, :].astype(BF16)
    edges[1] = rim[:, COLS - 1, :].astype(BF16)
    latent = lat_ref[...].astype(F32).reshape(T, C)
    first = jnp.sum(latent, axis=0, keepdims=True)
    second = jnp.sum(latent * latent, axis=0, keepdims=True)
    spot = iota((8, C), 0)
    stats[0] = jnp.where(spot == 0, first, jnp.where(spot == 1, second, 0.0))

    pl.semaphore_wait(barrier, len(partners))

    def shard(q, ia, ib):
        return wg.at[half, ring(q, 4) * 16 + ring(ia, 4) * sa + ring(ib, 4) * sb]

    def z_send(dq, step, slot):
        piece = shard(zl + dq, a, b)
        send(piece, piece, arr_wz.at[slot], at_z(step))

    def z_landed(dq, slot):
        landed(shard(zl + dq, a, b), arr_wz.at[slot])

    def a_send(dq, da, step, slot):
        piece = shard(zl + dq, a + da, b)
        send(piece, piece, arr_wa.at[dq, slot], at_a(step))

    def a_landed(dq, da, slot):
        landed(shard(zl + dq, a + da, b), arr_wa.at[dq, slot])

    def b_send(dq, da, db, step, slot):
        piece = shard(zl + dq, a + da, b + db)
        send(piece, piece, arr_wb.at[dq, da, slot], at_b(step))

    def b_landed(dq, da, db, slot):
        landed(shard(zl + dq, a + da, b + db), arr_wb.at[dq, da, slot])

    def spread(dq, da):
        b_send(dq, da, 0, 1, 0)
        b_send(dq, da, 0, -1, 1)

    def spread_on(dq, da):
        b_landed(dq, da, -1, 0)
        b_landed(dq, da, 1, 1)
        if (dq + da) % 2:
            b_send(dq, da, 1, -1, 2)
        else:
            b_send(dq, da, -1, 1, 2)

    def begin(dq):
        a_send(dq, 0, 1, 0)
        a_send(dq, 0, -1, 1)
        spread(dq, 0)

    def second_step(dq):
        a_landed(dq, 3, 0)
        a_landed(dq, 1, 1)
        if dq % 2:
            a_send(dq, 1, -1, 2)
        else:
            a_send(dq, 3, 1, 2)
        spread(dq, 3)
        spread(dq, 1)

    def third_step(dq):
        a_landed(dq, 2, 2)
        spread(dq, 2)

    send(stats.at[0], stats.at[1], arr_st.at[0], sibling)
    z_send(0, 1, 0)
    z_send(0, -1, 1)
    begin(0)
    send(edges.at[1], halo.at[0], arr_h.at[0], at_col(1))
    send(edges.at[0], halo.at[1], arr_h.at[1], at_col(-1))

    def strip(dz, mine, kv, part):
        slot = ring(zh + dz, 4) * 2 + (core if mine else 1 - core)
        return kvg.at[slot, kv, pl.ds(part * (T // 2), T // 2)]

    def own(kv, part):
        return kv_ref.at[kv, pl.ds(part * (T // 2), T // 2)]

    for kv in range(2):
        for part in range(2):
            send(own(kv, part), strip(0, True, kv, part), arr_k.at[0, kv, part], at_zh(1))
            send(own(1 - kv, part), strip(0, True, 1 - kv, part), arr_k.at[1, 1 - kv, part], at_zh(-1))
    for kv in range(2):
        for part in range(2):
            send(own(kv, part), strip(0, True, kv, part), arr_ks.at[0, kv, part], sibling)

    landed(stats.at[1], arr_st.at[0])
    stats[2] = stats[0] + stats[1]
    send(stats.at[2], stats.at[3], arr_st.at[1], at_zh(1))
    send(stats.at[2], stats.at[4], arr_st.at[2], at_zh(-1))
    send(stats.at[2], stats.at[5], arr_st.at[3], at_zh(2))

    second_step(0)
    z_landed(3, 0)
    z_landed(1, 1)

    @pl.when(core == 0)
    def _():
        piece = shard(zl + 1, a, b)
        copy(piece, piece, arr_wz.at[2], at_z(-1)).start()

    @pl.when(core == 1)
    def _():
        piece = shard(zl + 3, a, b)
        copy(piece, piece, arr_wz.at[2], at_z(1)).start()

    sent.append(copy(shard(zl + 1, a, b), shard(zl + 1, a, b), arr_wz.at[2], at_z(1)))
    begin(3)
    begin(1)
    third_step(0)
    z_landed(2, 2)
    begin(2)

    for slot in range(3):
        landed(stats.at[3 + slot], arr_st.at[1 + slot])
    sums = (stats[2] + stats[5]) + (stats[3] + stats[4])
    member = iota((C, 128), 0) - 40 * iota((C, 128), 1)
    member = jnp.where((member >= 0) & (member < 40), 1.0, 0.0)
    back = iota((128, C), 1) - 40 * iota((128, C), 0)
    back = jnp.where((back >= 0) & (back < 40), 1.0, 0.0)
    exact = lax.Precision.HIGHEST
    grouped = jnp.dot(sums, member, precision=exact, preferred_element_type=F32)
    grouped = jnp.dot(grouped, back, precision=exact, preferred_element_type=F32)
    count = T * STRIPS * (C // GROUPS)
    average = grouped[0:1] / count
    spread_of = grouped[1:2] / count - average * average
    factor = lax.rsqrt(spread_of + EPS)

    spread_on(0, 0)
    second_step(3)
    second_step(1)
    spread_on(0, 3)
    spread_on(0, 1)

    latent = lat_ref[...].astype(F32).reshape(T, C)
    normed = (latent - average) * factor * gain_ref[...] + shift_ref[...]
    fresh = (normed / (1.0 + jnp.exp(-normed))).astype(BF16).astype(F32)

    second_step(2)
    spread_on(3, 0)
    spread_on(1, 0)

    landed(halo.at[0], arr_h.at[0])
    landed(halo.at[1], arr_h.at[1])

    def rim_rows(side, present):
        cells = jnp.where(present, halo[side].astype(F32), 0.0)
        return jnp.broadcast_to(cells[:, None, :], (ROWS, COLS, C)).reshape(T, C)

    place = iota((T, C), 0) % COLS
    left = jnp.where(place == 0, rim_rows(0, col > 0), pltpu.roll(fresh, 1, 0))
    right = jnp.where(place == COLS - 1, rim_rows(1, col < STRIPS - 1), pltpu.roll(fresh, T - 1, 0))
    shifted = [left.astype(BF16), fresh.astype(BF16), right.astype(BF16)]

    third_step(3)
    third_step(1)
    spread_on(0, 2)
    spread_on(2, 0)

    for block in range(4):
        lanes = iota((C, 512), 1)
        within = lanes % 32
        base = (block * 16 + lanes // 32) * SHARD - iota((C, 512), 0)
        part = None
        for tap in range(3):
            inside = (within >= SHARD * tap) & (within < SHARD * (tap + 1))
            chosen = inside & (base + within - SHARD * tap == 0)
            chosen = jnp.where(chosen, 1.0, 0.0).astype(BF16)
            term = jnp.dot(shifted[tap], chosen, preferred_element_type=F32)
            part = term if part is None else part + term
        packed[block] = part.astype(BF16)
        if block == 0:
            third_step(2)
            spread_on(3, 3)
            spread_on(3, 1)
        if block == 1:
            spread_on(1, 3)
            spread_on(1, 1)
        if block == 2:
            spread_on(3, 2)
            spread_on(1, 2)
            spread_on(2, 3)
            spread_on(2, 1)
    spread_on(2, 2)

    def whole(dq, which):
        return wg.at[pl.ds(2 * which, 2), pl.ds(ring(zl + dq, 4) * 16, 16)]

    for dq in (0, 3, 1, 2):
        for da in range(4):
            b_landed(dq, da, 2, 2)
        send(whole(dq, core), whole(dq, core), arr_ws.at[dq], sibling)

    for part in range(2):
        landed(strip(-1, True, 0, part), arr_k.at[0, 0, part])
        send(strip(-1, True, 0, part), strip(-1, True, 0, part), arr_kf.at[0, part], at_zh(1))
        send(strip(-1, True, 0, part), strip(-1, True, 0, part), arr_ks.at[1, 0, part], sibling)
        landed(strip(1, True, 1, part), arr_k.at[1, 1, part])
        send(strip(1, True, 1, part), strip(1, True, 1, part), arr_kf.at[1, part], at_zh(-1))
        send(strip(1, True, 1, part), strip(1, True, 1, part), arr_ks.at[2, 1, part], sibling)

    for dq in (0, 3, 1, 2):
        landed(whole(dq, 1 - core), arr_ws.at[dq])

    conv_acc[...] = jnp.zeros_like(conv_acc)

    @pl.loop(0, 4)
    def _(block):
        cells = packed[block]
        for tap in range(3):
            weights = wg[tap, pl.ds(block * 16, 16)].reshape(512, C)
            conv_acc[tap] += jnp.dot(cells, weights, preferred_element_type=F32)

    take = iota((240, 256), 0)
    lanes = iota((240, 256), 1)
    tap_of = jnp.where(take >= 160, 2, jnp.where(take >= 80, 1, 0))
    channel = take - 80 * tap_of
    place = lanes % 32 - SHARD * tap_of
    pick = (place >= 0) & (place < SHARD) & (channel == SHARD * (lanes // 32) + place)
    pick = jnp.where(pick, 1.0, 0.0).astype(BF16)

    @pl.loop(0, 8)
    def _(block):
        part = wg[3, pl.ds(block * 8, 8)].reshape(256, C)
        part = jnp.dot(pick, part, preferred_element_type=F32).astype(BF16)
        for tap in range(3):
            wq[tap, pl.ds(pl.multiple_of(block * 80, 80), 80)] = part[80 * tap : 80 * (tap + 1)]

    blank = jnp.zeros((COLS, C), F32)
    above = jnp.concatenate([blank, conv_acc[0, : T - COLS]], axis=0)
    below = jnp.concatenate([conv_acc[2, COLS:], blank], axis=0)
    latent = lat_ref[...].astype(F32).reshape(T, C)
    block_out = (latent + (above + conv_acc[1] + below) + bias_ref[...]).astype(BF16)
    block_ref[...] = block_out.astype(F32).reshape(ROWS, COLS, C).astype(BF16)
    cells = block_out.astype(F32)
    centered = cells - jnp.mean(cells, axis=1, keepdims=True)
    variance = jnp.mean(centered * centered, axis=1, keepdims=True)
    cells = (centered * lax.rsqrt(variance + EPS) * again_ref[...]).astype(BF16)

    for tap in range(3):
        projected = jnp.dot(cells, wq[tap], preferred_element_type=F32).astype(BF16)
        if tap > 0:
            fkv_ref[tap - 1] = projected.astype(F32).reshape(ROWS, COLS, C).astype(BF16)
            kvg[col, tap - 1] = projected
        else:
            queries = projected.astype(F32) * HEAD_DIM ** -0.5
            low = iota((T, 128), 1) < HEAD_DIM
            for pair in range(PAIRS):
                two = queries[:, pair * 128 : (pair + 1) * 128]
                q2[pair, :T] = jnp.where(low, two, 0.0).astype(BF16)
                q2[pair, T:] = jnp.where(low, 0.0, two).astype(BF16)

    top[...] = jnp.full(top.shape, -1e30, F32)
    total[...] = jnp.zeros_like(total)
    accum[...] = jnp.zeros_like(accum)

    def attend(slot, start, size):
        @pl.loop(0, PAIRS)
        def _(pair):
            lanes = pl.ds(pl.multiple_of(pair * 128, 128), 128)
            keys = kvg[slot, 0, pl.ds(start, size), lanes]
            values = kvg[slot, 1, pl.ds(start, size), lanes]
            scores = lax.dot_general(
                q2[pair], keys, (((1,), (1,)), ((), ())), preferred_element_type=F32
            ) * LOG2E
            old = top[pair]
            new = jnp.maximum(old, jnp.max(scores, axis=1, keepdims=True))
            rescale = jnp.exp2(old - new)
            weights = jnp.exp2(scores - new[:, :1])
            total[pair] = total[pair] * rescale + jnp.sum(weights, axis=1, keepdims=True)
            accum[pair] = accum[pair] * rescale + jnp.dot(
                weights.astype(BF16), values, preferred_element_type=F32
            )
            top[pair] = new

    def position(dz, mine):
        return ring(zh + dz, 4) * 2 + (core if mine else 1 - core)

    attend(col, 0, T)
    for kv in range(2):
        for part in range(2):
            landed(strip(0, False, kv, part), arr_ks.at[0, kv, part])
    attend(position(0, False), 0, T)

    for part in range(2):
        landed(strip(-1, True, 1, part), arr_k.at[0, 1, part])
        send(strip(-1, True, 1, part), strip(-1, True, 1, part), arr_ks.at[1, 1, part], sibling)
        landed(strip(1, True, 0, part), arr_k.at[1, 0, part])
        send(strip(1, True, 0, part), strip(1, True, 0, part), arr_ks.at[2, 0, part], sibling)
    for index, dz in ((1, -1), (2, 1)):
        attend(position(dz, True), 0, T)
    for index, dz in ((1, -1), (2, 1)):
        for kv in range(2):
            for part in range(2):
                landed(strip(dz, False, kv, part), arr_ks.at[index, kv, part])
        attend(position(dz, False), 0, T)
    for part in range(2):
        for kv in range(2):
            landed(strip(2, True, kv, part), arr_kf.at[kv, part])
            send(strip(2, True, kv, part), strip(2, True, kv, part), arr_ks.at[3, kv, part], sibling)
        attend(position(2, True), part * (T // 2), T // 2)
        for kv in range(2):
            landed(strip(2, False, kv, part), arr_ks.at[3, kv, part])
        attend(position(2, False), part * (T // 2), T // 2)

    low = iota((T, 128), 1) < HEAD_DIM
    for pair in range(PAIRS):
        result = accum[pair] / total[pair]
        two = jnp.where(low, result[:T], result[T:])
        att_ref[:, :, pair * 128 : (pair + 1) * 128] = two.reshape(ROWS, COLS, 128).astype(BF16)

    for started in sent:
        started.wait_send()


def on_device(
    latent, stale_rim, stale_kv, norm_gain, norm_shift, conv_weight, conv_bias, attn_gain, qkv_weight
):
    taps = conv_weight.reshape(3, 3 * SHARD, C)
    projections = qkv_weight.reshape(SHARD, 3, C).transpose(1, 0, 2).reshape(1, 3 * SHARD, C)
    weights = jnp.concatenate([taps, projections], axis=0)
    weights = jnp.pad(weights, ((0, 0), (0, 2), (0, 0)))
    vmem = pl.BlockSpec(memory_space=pltpu.VMEM)
    dma = pltpu.SemaphoreType.DMA
    cells = jax.ShapeDtypeStruct((ROWS, COLS, C), BF16)
    block, attended, fresh_kv = pl.pallas_call(
        kernel,
        out_shape=(cells, cells, jax.ShapeDtypeStruct((2, ROWS, COLS, C), BF16)),
        in_specs=[vmem, vmem, pl.BlockSpec(memory_space=pl.ANY)] + [vmem] * 5,
        out_specs=(vmem, vmem, vmem),
        scratch_shapes=[
            pltpu.VMEM((4, SHARDS, 32, C), BF16),
            pltpu.VMEM((STRIPS, 2, T, C), BF16),
            pltpu.VMEM((6, 8, C), F32),
            pltpu.VMEM((2, ROWS, C), BF16),
            pltpu.VMEM((2, ROWS, C), BF16),
            pltpu.VMEM((4, T, 512), BF16),
            pltpu.VMEM((3, T, C), F32),
            pltpu.VMEM((3, C, C), BF16),
            pltpu.VMEM((PAIRS, 2 * T, 128), BF16),
            pltpu.VMEM((PAIRS, 2 * T, 128), F32),
            pltpu.VMEM((PAIRS, 2 * T, 128), F32),
            pltpu.VMEM((PAIRS, 2 * T, 128), F32),
            dma((128,)),
            dma((3,)),
            dma((4, 3)),
            dma((4, 4, 3)),
            dma((4,)),
            dma((4,)),
            dma((2,)),
            dma((2, 2, 2)),
            dma((2, 2)),
            dma((4, 2, 2)),
        ],
        compiler_params=pltpu.CompilerParams(
            collective_id=0, has_side_effects=True, vmem_limit_bytes=56 * 2**20
        ),
    )(
        latent.reshape(ROWS, COLS, C),
        stale_rim.reshape(ROWS, COLS, C),
        stale_kv.reshape(2, T, C),
        norm_gain.reshape(1, C),
        norm_shift.reshape(1, C),
        weights,
        conv_bias.reshape(1, C),
        attn_gain.reshape(1, C),
    )
    shape = latent.shape
    return block.reshape(shape), attended.reshape(shape), fresh_kv.reshape((2,) + shape)


def solution(mesh):
    cells = P("row", None, "col", None)
    pairs = P(None, "row", None, "col", None)
    return jax.shard_map(
        on_device,
        mesh=mesh,
        in_specs=(cells, cells, pairs, P(), P(), P(None, "row", None), P(), P(), P("row", None)),
        out_specs=(cells, cells, pairs),
        check_vma=False,
    )
```

```python
import jax
import jax.numpy as jnp
from jax import lax
from jax.experimental import pallas as pl
from jax.experimental.pallas import tpu as pltpu
from jax.sharding import PartitionSpec as P

HEADS = 10
HEAD_DIM = 64
GROUPS = 16
C = 640
ROWS = 32
COLS = 8
T = ROWS * COLS
STRIPS = 8
SHARD = 10
SHARDS = 64
PAIRS = 5
EPS = 1e-05
LOG2E = 1.4426950408889634
MESH = pl.DeviceIdType.MESH
F32 = jnp.float32
BF16 = jnp.bfloat16


def iota(shape, dim):
    return lax.broadcasted_iota(jnp.int32, shape, dim)


def part_of(q, blocks):
    low = iota((T, 128), 1) < HEAD_DIM
    scaled = q.astype(F32) * HEAD_DIM ** -0.5
    found = []
    for head in range(2):
        mine = jnp.where(low, scaled, 0.0) if head == 0 else jnp.where(low, 0.0, scaled)
        mine = mine.astype(BF16)
        scores = [
            lax.dot_general(mine, keys(), (((1,), (1,)), ((), ())), preferred_element_type=F32)
            for keys, _ in blocks
        ]
        best = scores[0]
        for score in scores[1:]:
            best = jnp.maximum(best, score)
        top = jnp.max(best, axis=1, keepdims=True) * LOG2E
        total = result = None
        for score, (_, values) in zip(scores, blocks):
            weights = jnp.exp2(score * LOG2E - top)
            term = jnp.dot(weights.astype(BF16), values(), preferred_element_type=F32)
            total = weights if total is None else total + weights
            result = term if result is None else result + term
        total = jnp.sum(total, axis=1, keepdims=True)
        found.append((result / total, top + jnp.log(total) * LOG2E))
    result = jnp.where(low, found[0][0], found[1][0])
    return result, jnp.where(low, found[0][1], found[1][1])


def kernel(
    lat_ref, rim_ref, kv_ref, gain_ref, shift_ref, w_ref, bias_ref, again_ref,
    block_ref, att_ref, fkv_ref,
    wg, kvp, kv4, stats, edges, halo, packed, conv_acc, wq,
    qs, qin, kf, fresh_o, fresh_l, rout, sout, rin, sin,
    sems, own_sem, arr_wz, arr_wa, arr_wb, arr_ws, arr_st, arr_h,
    arr_p, arr_4, arr_ps, arr_4s, arr_q, arr_r, arr_s,
):
    row, col = lax.axis_index("row"), lax.axis_index("col")
    zl, xy = lax.div(row, 16), lax.rem(row, 16)
    x, y = lax.div(xy, 4), lax.rem(xy, 4)
    zh, core = lax.div(col, 2), lax.rem(col, 2)
    a, b = x + core * (y - x), y + core * (x - y)
    sa, sb = 4 - 3 * core, 1 + 3 * core

    def ring(value, size):
        return lax.rem(value + size, size)

    def at_a(step):
        return (zl * 16 + ring(a + step, 4) * sa + b * sb, col)

    def at_b(step):
        return (zl * 16 + a * sa + ring(b + step, 4) * sb, col)

    def at_z(step):
        z = ring(zh * 4 + zl + step, 16)
        return (lax.rem(z, 4) * 16 + xy, lax.div(z, 4) * 2 + core)

    def at_zh(step):
        return (row, ring(zh + step, 4) * 2 + core)

    def at_col(step):
        return (row, ring(col + step, 8))

    sibling = (row, col + 1 - 2 * core)
    cross = at_col(2 * core - 1)

    barrier = pltpu.get_barrier_semaphore()
    partners = [at_a(1), at_a(-1), at_a(2), at_b(1), at_b(-1), at_z(1), at_z(-1), at_z(4 * core - 2)]
    partners += [at_zh(1), at_zh(-1), at_zh(2), sibling, cross]
    for partner in partners:
        pl.semaphore_signal(barrier, inc=1, device_id=partner, device_id_type=MESH)

    sent = []

    def copy(src, dst, arrived, device, index=None):
        index = len(sent) if index is None else index
        return pltpu.make_async_remote_copy(
            src_ref=src, dst_ref=dst, send_sem=sems.at[index], recv_sem=arrived,
            device_id=device, device_id_type=MESH,
        )

    def send(src, dst, arrived, device):
        started = copy(src, dst, arrived, device)
        started.start()
        sent.append(started)

    def landed(dst, arrived):
        copy(dst, dst, arrived, sibling, 0).wait_recv()

    half = pl.ds(2 * core, 2)

    def lanes_of(pair):
        return pl.ds(pl.multiple_of(pair * 128, 128), 128)

    wg[half, pl.ds(row, 1)] = w_ref[half][:, None]
    rim = rim_ref[...].astype(F32)
    edges[0] = rim[:, 0, :].astype(BF16)
    edges[1] = rim[:, COLS - 1, :].astype(BF16)
    latent = lat_ref[...].astype(F32).reshape(T, C)
    first = jnp.sum(latent, axis=0, keepdims=True)
    second = jnp.sum(latent * latent, axis=0, keepdims=True)
    spot = iota((8, C), 0)
    stats[0] = jnp.where(spot == 0, first, jnp.where(spot == 1, second, 0.0))

    keep = pltpu.make_async_copy(kv_ref.at[:, :, lanes_of(zh)], kvp.at[col], own_sem.at[0])
    keep.start()

    pl.semaphore_wait(barrier, len(partners))

    def shard(q, ia, ib):
        return wg.at[half, ring(q, 4) * 16 + ring(ia, 4) * sa + ring(ib, 4) * sb]

    def z_send(step, slot):
        piece = shard(zl, a, b)
        send(piece, piece, arr_wz.at[slot], at_z(step))

    def z_landed(dq, slot):
        landed(shard(zl + dq, a, b), arr_wz.at[slot])

    def b_send(dq, da, db, step, slot):
        piece = shard(zl + dq, a + da, b + db)
        send(piece, piece, arr_wb.at[dq, da, slot], at_b(step))

    def b_landed(dq, da, db, slot):
        landed(shard(zl + dq, a + da, b + db), arr_wb.at[dq, da, slot])

    def spread(dq, da):
        b_send(dq, da, 0, 1, 0)
        b_send(dq, da, 0, -1, 1)

    def spread_on(dq, da):
        b_landed(dq, da, -1, 0)
        b_landed(dq, da, 1, 1)
        if (dq + da) % 2:
            b_send(dq, da, 1, -1, 2)
        else:
            b_send(dq, da, -1, 1, 2)

    def a_start(dq):
        piece = shard(zl + dq, a, b)
        for slot, step in ((0, 1), (1, -1), (2, 2)):
            send(piece, piece, arr_wa.at[dq, slot], at_a(step))
        spread(dq, 0)

    def a_next(dq):
        for slot, da in ((0, 3), (1, 1)):
            landed(shard(zl + dq, a + da, b), arr_wa.at[dq, slot])
            spread(dq, da)

    def a_last(dq):
        landed(shard(zl + dq, a + 2, b), arr_wa.at[dq, 2])
        spread(dq, 2)

    def whole(dq, which):
        return wg.at[pl.ds(2 * which, 2), pl.ds(ring(zl + dq, 4) * 16, 16)]

    def finish(dq):
        for da in range(4):
            b_landed(dq, da, 2, 2)
        send(whole(dq, core), whole(dq, core), arr_ws.at[dq], sibling)

    def place_of(dz, mine=True):
        return ring(zh + dz, 4) * 2 + (core if mine else 1 - core)

    send(stats.at[0], stats.at[1], arr_st.at[0], sibling)
    z_send(1, 0)
    z_send(-1, 1)
    z_send(2 - 4 * core, 2)
    a_start(0)
    send(edges.at[1], halo.at[0], arr_h.at[0], at_col(1))
    send(edges.at[0], halo.at[1], arr_h.at[1], at_col(-1))

    landed(stats.at[1], arr_st.at[0])
    stats[2] = stats[0] + stats[1]
    send(stats.at[2], stats.at[3], arr_st.at[1], at_zh(1))
    send(stats.at[2], stats.at[4], arr_st.at[2], at_zh(-1))
    send(stats.at[2], stats.at[5], arr_st.at[3], at_zh(2))

    for dz in (1, 3, 2):
        send(kv_ref.at[:, :, lanes_of(ring(zh + dz, 4))], kvp.at[col], arr_p.at[4 - dz], at_zh(dz))
    last = lanes_of(PAIRS - 1)
    for kv in range(2):
        send(kv_ref.at[kv, :, last], kv4.at[col, kv], arr_4.at[3, kv], at_zh(1))
        send(kv_ref.at[1 - kv, :, last], kv4.at[col, 1 - kv], arr_4.at[1, 1 - kv], at_zh(-1))
    send(kv_ref.at[:, :, lanes_of(zh)], kvp.at[col], arr_ps.at[0], sibling)
    send(kv_ref.at[:, :, last], kv4.at[col], arr_4s.at[0], sibling)

    a_next(0)
    z_landed(3, 0)
    a_start(3)
    z_landed(1, 1)
    a_start(1)
    a_last(0)
    z_landed(2, 2)
    a_start(2)
    spread_on(0, 0)

    a_next(3)
    a_next(1)
    spread_on(0, 3)
    spread_on(0, 1)
    for slot in range(3):
        landed(stats.at[3 + slot], arr_st.at[1 + slot])
    sums = (stats[2] + stats[5]) + (stats[3] + stats[4])
    member = iota((C, 128), 0) - 40 * iota((C, 128), 1)
    member = jnp.where((member >= 0) & (member < 40), 1.0, 0.0)
    back = iota((128, C), 1) - 40 * iota((128, C), 0)
    back = jnp.where((back >= 0) & (back < 40), 1.0, 0.0)
    exact = lax.Precision.HIGHEST
    grouped = jnp.dot(sums, member, precision=exact, preferred_element_type=F32)
    grouped = jnp.dot(grouped, back, precision=exact, preferred_element_type=F32)
    count = T * STRIPS * (C // GROUPS)
    average = grouped[0:1] / count
    spread_of = grouped[1:2] / count - average * average
    factor = lax.rsqrt(spread_of + EPS)


    latent = lat_ref[...].astype(F32).reshape(T, C)
    normed = (latent - average) * factor * gain_ref[...].reshape(1, C) + shift_ref[...].reshape(1, C)
    fresh = (normed / (1.0 + jnp.exp(-normed))).astype(BF16).astype(F32)

    a_last(3)
    a_last(1)
    a_next(2)
    spread_on(3, 0)
    spread_on(1, 0)

    landed(halo.at[0], arr_h.at[0])
    landed(halo.at[1], arr_h.at[1])

    def rim_rows(side, present):
        cells = jnp.where(present, halo[side].astype(F32), 0.0)
        return jnp.broadcast_to(cells[:, None, :], (ROWS, COLS, C)).reshape(T, C)

    place = iota((T, C), 0) & (COLS - 1)
    left = jnp.where(place == 0, rim_rows(0, col > 0), pltpu.roll(fresh, 1, 0))
    right = jnp.where(place == COLS - 1, rim_rows(1, col < STRIPS - 1), pltpu.roll(fresh, T - 1, 0))
    shifted = [left.astype(BF16), fresh.astype(BF16), right.astype(BF16)]

    a_last(2)
    spread_on(0, 2)
    spread_on(2, 0)

    for block in range(4):
        lanes = iota((1, 512), 1)
        within = lanes & 31
        channel = 32 * block + SHARD * (lanes >> 5) + within
        cells = slice(128 * block, 128 * block + 256)
        part = None
        for tap in range(3):
            inside = (within >= SHARD * tap) & (within < SHARD * (tap + 1))
            wanted = jnp.where(inside, channel - SHARD * tap, -1)
            chosen = jnp.where(iota((256, 512), 0) == wanted, 1.0, 0.0).astype(BF16)
            term = jnp.dot(shifted[tap][:, cells], chosen, preferred_element_type=F32)
            part = term if part is None else part + term
        packed[block] = part.astype(BF16)
        if block == 0:
            spread_on(3, 3)
            spread_on(3, 1)
            spread_on(1, 3)
            spread_on(1, 1)
        if block == 1:
            spread_on(3, 2)
            spread_on(1, 2)
        if block == 2:
            spread_on(2, 3)
            spread_on(2, 1)
    finish(0)
    spread_on(2, 2)

    take = iota((240, 256), 0)
    lanes = iota((240, 256), 1)
    tap_of = jnp.where(take >= 160, 2, jnp.where(take >= 80, 1, 0))
    channel = take - 80 * tap_of
    place = (lanes & 31) - SHARD * tap_of
    pick = (place >= 0) & (place < SHARD) & (channel == SHARD * (lanes >> 5) + place)
    pick = jnp.where(pick, 1.0, 0.0).astype(BF16)


    conv_acc[...] = jnp.zeros_like(conv_acc)

    def multiply(dq):
        block = ring(zl + dq, 4)
        landed(whole(dq, 1 - core), arr_ws.at[dq])
        cells = packed[block]
        for tap in range(3):
            weights = wg[tap, pl.ds(block * 16, 16)].reshape(512, C)
            conv_acc[tap] += jnp.dot(cells, weights, preferred_element_type=F32)
        for part in range(2):
            rows = wg[3, pl.ds(block * 16 + part * 8, 8)].reshape(256, C)
            rows = jnp.dot(pick, rows, preferred_element_type=F32).astype(BF16)
            start = pl.multiple_of(block * 160 + part * 80, 80)
            for tap in range(3):
                wq[tap, pl.ds(start, 80)] = rows[80 * tap : 80 * (tap + 1)]

    def pass_on(dz):
        landed(kvp.at[place_of(dz)], arr_p.at[dz])
        send(kvp.at[place_of(dz)], kvp.at[place_of(dz)], arr_ps.at[dz], sibling)

    finish(3)
    multiply(0)
    finish(1)
    multiply(3)
    finish(2)
    pass_on(3)
    pass_on(1)
    multiply(1)
    multiply(2)

    blank = jnp.zeros((COLS, C), F32)
    above = jnp.concatenate([blank, conv_acc[0, : T - COLS]], axis=0)
    below = jnp.concatenate([conv_acc[2, COLS:], blank], axis=0)
    latent = lat_ref[...].astype(F32).reshape(T, C)
    block_out = (latent + (above + conv_acc[1] + below) + bias_ref[...].reshape(1, C)).astype(BF16)
    block_ref[...] = block_out.astype(F32).reshape(ROWS, COLS, C).astype(BF16)
    cells = block_out.astype(F32)
    centered = cells - jnp.mean(cells, axis=1, keepdims=True)
    variance = jnp.mean(centered * centered, axis=1, keepdims=True)
    cells = (centered * lax.rsqrt(variance + EPS) * again_ref[...].reshape(1, C).reshape(1, C)).astype(BF16)

    queries = jnp.dot(cells, wq[0], preferred_element_type=F32).astype(BF16)
    for pair in range(PAIRS):
        qs[pair] = queries[:, pair * 128 : (pair + 1) * 128]
    qin[zh] = qs[zh]
    for dz in (2, 1, 3):
        send(qs.at[ring(zh + dz, 4)], qin.at[zh], arr_q.at[zh], at_zh(dz))
    for tap in (1, 2):
        projected = jnp.dot(cells, wq[tap], preferred_element_type=F32).astype(BF16)
        fkv_ref[tap - 1] = projected.astype(F32).reshape(ROWS, COLS, C).astype(BF16)
        kf[tap - 1] = projected

    landed(kv4.at[place_of(3), 0], arr_4.at[3, 0])
    send(kv4.at[place_of(3), 0], kv4.at[place_of(3), 0], arr_4.at[2, 0], at_zh(1))
    landed(kv4.at[place_of(1), 1], arr_4.at[1, 1])
    send(kv4.at[place_of(1), 1], kv4.at[place_of(1), 1], arr_4.at[2, 1], at_zh(-1))
    landed(kv4.at[place_of(3), 1], arr_4.at[3, 1])
    landed(kv4.at[place_of(1), 0], arr_4.at[1, 0])
    for dz in (3, 1):
        send(kv4.at[place_of(dz)], kv4.at[place_of(dz)], arr_4s.at[dz], sibling)
    pass_on(2)
    keep.wait()

    @pl.loop(0, PAIRS - 1)
    def _(pair):
        lanes = lanes_of(pair)
        result, level = part_of(qs[pair], [(lambda: kf[0, :, lanes], lambda: kf[1, :, lanes])])
        fresh_o[pair] = result
        fresh_l[pair] = level

    for dz in range(4):
        landed(kvp.at[place_of(dz, False)], arr_ps.at[dz])

    def strips_but(mine, ref):
        def block(step, kv):
            return lambda: ref[lax.rem(mine + 1 + step, STRIPS), kv]

        return [(block(step, 0), block(step, 1)) for step in range(STRIPS - 1)]

    def give(turn, dz):
        source = ring(zh + dz, 4)
        results = copy(rout.at[source], rin.at[zh], arr_r.at[zh], at_zh(dz), 120 + turn)
        levels = copy(sout.at[source], sin.at[zh], arr_s.at[zh], at_zh(dz), 124 + turn)
        return results, levels

    @pl.loop(0, 4)
    def _(turn):
        dz = jnp.where(turn == 0, 1, jnp.where(turn == 1, 3, jnp.where(turn == 2, 2, 0)))
        source = ring(zh + dz, 4)

        @pl.when(turn < 3)
        def _():
            landed(qin.at[source], arr_q.at[source])

        result, level = part_of(qin[source], strips_but(source * 2 + core, kvp))
        level = level.T
        level = jnp.where(iota((8, T), 0) == 0, level[0:1], level[HEAD_DIM : HEAD_DIM + 1])

        @pl.when(turn < 3)
        def _():
            rout[source] = result.astype(BF16)
            sout[source] = level
            for outgoing in give(turn, dz):
                outgoing.start()

        @pl.when(turn == 3)
        def _():
            rin[zh] = result.astype(BF16)
            sin[zh] = level

    def put(pair, result):
        att_ref[:, :, pair * 128 : (pair + 1) * 128] = result.reshape(ROWS, COLS, 128).astype(BF16)

    furthest = kv4.at[place_of(2)]
    for kv in range(2):
        landed(kv4.at[place_of(2), kv], arr_4.at[2, kv])
    send(furthest, furthest, arr_4s.at[2], sibling)
    for dz in range(4):
        landed(kv4.at[place_of(dz, False)], arr_4s.at[dz])
    fresh_pair = (lambda: kf[0, :, last], lambda: kf[1, :, last])
    put(PAIRS - 1, part_of(qs[PAIRS - 1], [fresh_pair] + strips_but(col, kv4))[0])

    for dz in (1, 3, 2):
        landed(rin.at[ring(zh + dz, 4)], arr_r.at[ring(zh + dz, 4)])
        landed(sin.at[ring(zh + dz, 4)], arr_s.at[ring(zh + dz, 4)])
    for pair in range(PAIRS - 1):
        level = jnp.where(iota((128, T), 0) < HEAD_DIM, sin[pair, 0:1], sin[pair, 1:2]).T
        most = jnp.maximum(level, fresh_l[pair])
        old, new = jnp.exp2(level - most), jnp.exp2(fresh_l[pair] - most)
        put(pair, (rin[pair].astype(F32) * old + fresh_o[pair] * new) / (old + new))

    for turn, dz in enumerate((1, 3, 2)):
        for outgoing in give(turn, dz):
            outgoing.wait_send()
    for started in sent:
        started.wait_send()


def on_device(
    latent, stale_rim, stale_kv, norm_gain, norm_shift, conv_weight, conv_bias, attn_gain, qkv_weight
):
    taps = conv_weight.reshape(3, 3 * SHARD, C)
    projections = qkv_weight.reshape(SHARD, 3, C).transpose(1, 0, 2).reshape(1, 3 * SHARD, C)
    weights = jnp.concatenate([taps, projections], axis=0)
    weights = jnp.pad(weights, ((0, 0), (0, 2), (0, 0)))
    vmem = pl.BlockSpec(memory_space=pltpu.VMEM)
    dma = pltpu.SemaphoreType.DMA
    cells = jax.ShapeDtypeStruct((ROWS, COLS, C), BF16)
    block, attended, fresh_kv = pl.pallas_call(
        kernel,
        out_shape=(cells, cells, jax.ShapeDtypeStruct((2, ROWS, COLS, C), BF16)),
        in_specs=[vmem, vmem, pl.BlockSpec(memory_space=pl.ANY)] + [vmem] * 5,
        out_specs=(vmem, vmem, vmem),
        scratch_shapes=[
            pltpu.VMEM((4, SHARDS, 32, C), BF16),
            pltpu.VMEM((STRIPS, 2, T, 128), BF16),
            pltpu.VMEM((STRIPS, 2, T, 128), BF16),
            pltpu.VMEM((6, 8, C), F32),
            pltpu.VMEM((2, ROWS, C), BF16),
            pltpu.VMEM((2, ROWS, C), BF16),
            pltpu.VMEM((4, T, 512), BF16),
            pltpu.VMEM((3, T, C), F32),
            pltpu.VMEM((3, C, C), BF16),
            pltpu.VMEM((PAIRS, T, 128), BF16),
            pltpu.VMEM((4, T, 128), BF16),
            pltpu.VMEM((2, T, C), BF16),
            pltpu.VMEM((4, T, 128), F32),
            pltpu.VMEM((4, T, 128), F32),
            pltpu.VMEM((4, T, 128), BF16),
            pltpu.VMEM((4, 8, T), F32),
            pltpu.VMEM((4, T, 128), BF16),
            pltpu.VMEM((4, 8, T), F32),
            dma((128,)),
            dma((1,)),
            dma((3,)),
            dma((4, 3)),
            dma((4, 4, 3)),
            dma((4,)),
            dma((4,)),
            dma((2,)),
            dma((4,)),
            dma((4, 2)),
            dma((4,)),
            dma((4,)),
            dma((4,)),
            dma((4,)),
            dma((4,)),
        ],
        compiler_params=pltpu.CompilerParams(
            collective_id=0, has_side_effects=True, vmem_limit_bytes=56 * 2**20
        ),
    )(
        latent.reshape(ROWS, COLS, C),
        stale_rim.reshape(ROWS, COLS, C),
        stale_kv.reshape(2, T, C),
        norm_gain,
        norm_shift,
        weights,
        conv_bias,
        attn_gain,
    )
    shape = latent.shape
    return block.reshape(shape), attended.reshape(shape), fresh_kv.reshape((2,) + shape)


def solution(mesh):
    cells = P("row", None, "col", None)
    pairs = P(None, "row", None, "col", None)
    return jax.shard_map(
        on_device,
        mesh=mesh,
        in_specs=(cells, cells, pairs, P(), P(), P(None, "row", None), P(), P(), P("row", None)),
        out_specs=(cells, cells, pairs),
        check_vma=False,
    )
```

```python
import jax
import jax.numpy as jnp
from jax import lax
from jax.experimental import pallas as pl
from jax.experimental.pallas import tpu as pltpu
from jax.sharding import PartitionSpec as P

HEADS = 10
HEAD_DIM = 64
GROUPS = 16
C = 640
ROWS = 32
COLS = 8
T = ROWS * COLS
STRIPS = 8
SHARD = 10
SHARDS = 64
PAIRS = 5
EPS = 1e-05
LOG2E = 1.4426950408889634
MESH = pl.DeviceIdType.MESH
F32 = jnp.float32
BF16 = jnp.bfloat16


def iota(shape, dim):
    return lax.broadcasted_iota(jnp.int32, shape, dim)


def part_of(q, blocks):
    low = iota((T, 128), 1) < HEAD_DIM
    scaled = q.astype(F32) * HEAD_DIM ** -0.5
    found = []
    for head in range(2):
        mine = jnp.where(low, scaled, 0.0) if head == 0 else jnp.where(low, 0.0, scaled)
        mine = mine.astype(BF16)
        scores = [
            lax.dot_general(mine, keys(), (((1,), (1,)), ((), ())), preferred_element_type=F32)
            for keys, _ in blocks
        ]
        best = scores[0]
        for score in scores[1:]:
            best = jnp.maximum(best, score)
        top = jnp.max(best, axis=1, keepdims=True) * LOG2E
        total = result = None
        for score, (_, values) in zip(scores, blocks):
            weights = jnp.exp2(score * LOG2E - top)
            term = jnp.dot(weights.astype(BF16), values(), preferred_element_type=F32)
            total = weights if total is None else total + weights
            result = term if result is None else result + term
        total = jnp.sum(total, axis=1, keepdims=True)
        found.append((result / total, top + jnp.log(total) * LOG2E))
    result = jnp.where(low, found[0][0], found[1][0])
    return result, jnp.where(low, found[0][1], found[1][1])


def kernel(
    lat_ref, rim_ref, kv_ref, gain_ref, shift_ref, w_ref, bias_ref, again_ref,
    block_ref, att_ref, fkv_ref,
    wg, kvp, kv4, stats, edges, halo, packed, conv_acc, wq,
    qs, qin, kf, fresh_o, fresh_l, rout, sout, rin, sin,
    sems, own_sem, arr_wz, arr_wa, arr_wb, arr_ws, arr_st, arr_h,
    arr_p, arr_4, arr_ps, arr_4s, arr_q, arr_r, arr_s,
):
    row, col = lax.axis_index("row"), lax.axis_index("col")
    zl, xy = lax.div(row, 16), lax.rem(row, 16)
    x, y = lax.div(xy, 4), lax.rem(xy, 4)
    zh, core = lax.div(col, 2), lax.rem(col, 2)
    a, b = x + core * (y - x), y + core * (x - y)
    sa, sb = 4 - 3 * core, 1 + 3 * core

    def ring(value, size):
        return lax.rem(value + size, size)

    def at_a(step):
        return (zl * 16 + ring(a + step, 4) * sa + b * sb, col)

    def at_b(step):
        return (zl * 16 + a * sa + ring(b + step, 4) * sb, col)

    def at_z(step):
        z = ring(zh * 4 + zl + step, 16)
        return (lax.rem(z, 4) * 16 + xy, lax.div(z, 4) * 2 + core)

    def at_zh(step):
        return (row, ring(zh + step, 4) * 2 + core)

    def at_col(step):
        return (row, ring(col + step, 8))

    sibling = (row, col + 1 - 2 * core)

    barrier = pltpu.get_barrier_semaphore()
    partners = [at_a(1), at_a(-1), at_a(2), at_b(1), at_b(-1), at_z(1), at_z(-1), at_z(4 * core - 2)]
    partners += [at_col(step) for step in range(1, STRIPS)]
    for partner in partners:
        pl.semaphore_signal(barrier, inc=1, device_id=partner, device_id_type=MESH)

    sent = []

    def copy(src, dst, arrived, device, index=None):
        index = len(sent) if index is None else index
        return pltpu.make_async_remote_copy(
            src_ref=src, dst_ref=dst, send_sem=sems.at[index], recv_sem=arrived,
            device_id=device, device_id_type=MESH,
        )

    def send(src, dst, arrived, device):
        started = copy(src, dst, arrived, device)
        started.start()
        sent.append(started)

    def landed(dst, arrived):
        copy(dst, dst, arrived, sibling, 0).wait_recv()

    half = pl.ds(2 * core, 2)

    def lanes_of(pair):
        return pl.ds(pl.multiple_of(pair * 128, 128), 128)

    wg[half, pl.ds(row, 1)] = w_ref[half][:, None]
    rim = rim_ref[...].astype(F32)
    edges[0] = rim[:, 0, :].astype(BF16)
    edges[1] = rim[:, COLS - 1, :].astype(BF16)
    latent = lat_ref[...].astype(F32).reshape(T, C)
    first = jnp.sum(latent, axis=0, keepdims=True)
    second = jnp.sum(latent * latent, axis=0, keepdims=True)
    spot = iota((8, C), 0)
    member = iota((C, 128), 0) - 40 * iota((C, 128), 1)
    member = jnp.where((member >= 0) & (member < 40), 1.0, 0.0)
    exact = lax.Precision.HIGHEST
    stats[col] = jnp.dot(
        jnp.where(spot == 0, first, jnp.where(spot == 1, second, 0.0)), member,
        precision=exact, preferred_element_type=F32,
    )

    kept = [
        pltpu.make_async_copy(kv_ref.at[:, :, lanes_of(ring(zh - which, 4))], kvp.at[which, col], own_sem.at[which])
        for which in range(2)
    ]
    for keep in kept:
        keep.start()

    pl.semaphore_wait(barrier, len(partners))

    def shard(q, ia, ib):
        return wg.at[half, ring(q, 4) * 16 + ring(ia, 4) * sa + ring(ib, 4) * sb]

    def z_send(step, slot):
        piece = shard(zl, a, b)
        send(piece, piece, arr_wz.at[slot], at_z(step))

    def z_landed(dq, slot):
        landed(shard(zl + dq, a, b), arr_wz.at[slot])

    def b_send(dq, da, db, step, slot):
        piece = shard(zl + dq, a + da, b + db)
        send(piece, piece, arr_wb.at[dq, da, slot], at_b(step))

    def b_landed(dq, da, db, slot):
        landed(shard(zl + dq, a + da, b + db), arr_wb.at[dq, da, slot])

    def spread(dq, da):
        b_send(dq, da, 0, 1, 0)
        b_send(dq, da, 0, -1, 1)

    def spread_on(dq, da):
        b_landed(dq, da, -1, 0)
        b_landed(dq, da, 1, 1)
        if (dq + da) % 2:
            b_send(dq, da, 1, -1, 2)
        else:
            b_send(dq, da, -1, 1, 2)

    def a_start(dq):
        piece = shard(zl + dq, a, b)
        for slot, step in ((0, 1), (1, -1), (2, 2)):
            send(piece, piece, arr_wa.at[dq, slot], at_a(step))
        spread(dq, 0)

    def a_next(dq):
        for slot, da in ((0, 3), (1, 1)):
            landed(shard(zl + dq, a + da, b), arr_wa.at[dq, slot])
            spread(dq, da)

    def a_last(dq):
        landed(shard(zl + dq, a + 2, b), arr_wa.at[dq, 2])
        spread(dq, 2)

    def whole(dq, which):
        return wg.at[pl.ds(2 * which, 2), pl.ds(ring(zl + dq, 4) * 16, 16)]

    def finish(dq):
        for da in range(4):
            b_landed(dq, da, 2, 2)
        send(whole(dq, core), whole(dq, core), arr_ws.at[dq], sibling)

    def place_of(dz, mine=True):
        return ring(zh + dz, 4) * 2 + (core if mine else 1 - core)

    for step in range(1, STRIPS):
        send(stats.at[col], stats.at[col], arr_st.at[step], at_col(step))
    z_send(1, 0)
    z_send(-1, 1)
    z_send(2 - 4 * core, 2)
    a_start(0)
    send(edges.at[1], halo.at[0], arr_h.at[0], at_col(1))
    send(edges.at[0], halo.at[1], arr_h.at[1], at_col(-1))

    def pair_of(dz):
        return kv_ref.at[:, :, lanes_of(ring(zh + dz, 4))]

    send(pair_of(1), kvp.at[0, col], arr_p.at[0, 3], at_zh(1))
    send(pair_of(-2), kvp.at[1, col], arr_p.at[1, 1], at_zh(-1))
    send(pair_of(0), kvp.at[1, col], arr_p.at[1, 3], at_zh(1))
    send(pair_of(-1), kvp.at[0, col], arr_p.at[0, 1], at_zh(-1))
    last = lanes_of(PAIRS - 1)
    send(pair_of(0), kvp.at[0, col], arr_ps.at[0], sibling)
    send(pair_of(-1), kvp.at[1, col], arr_ps.at[4], sibling)
    send(kv_ref.at[:, :, last], kv4.at[col], arr_4s.at[0], sibling)

    a_next(0)
    z_landed(3, 0)
    a_start(3)
    z_landed(1, 1)
    a_start(1)
    a_last(0)
    z_landed(2, 2)
    a_start(2)
    spread_on(0, 0)

    a_next(3)
    a_next(1)
    spread_on(0, 3)
    spread_on(0, 1)
    for step in range(1, STRIPS):
        landed(stats.at[ring(col - step, STRIPS)], arr_st.at[step])
    sums = stats[0]
    for strip in range(1, STRIPS):
        sums = sums + stats[strip]
    back = iota((128, C), 1) - 40 * iota((128, C), 0)
    back = jnp.where((back >= 0) & (back < 40), 1.0, 0.0)
    grouped = jnp.dot(sums, back, precision=exact, preferred_element_type=F32)
    count = T * STRIPS * (C // GROUPS)
    average = grouped[0:1] / count
    spread_of = grouped[1:2] / count - average * average
    factor = lax.rsqrt(spread_of + EPS)


    latent = lat_ref[...].astype(F32).reshape(T, C)
    normed = (latent - average) * factor * gain_ref[...].reshape(1, C) + shift_ref[...].reshape(1, C)
    fresh = (normed / (1.0 + jnp.exp(-normed))).astype(BF16).astype(F32)

    a_last(3)
    a_last(1)
    a_next(2)
    spread_on(3, 0)
    spread_on(1, 0)

    landed(halo.at[0], arr_h.at[0])
    landed(halo.at[1], arr_h.at[1])

    def rim_rows(side, present):
        cells = jnp.where(present, halo[side].astype(F32), 0.0)
        return jnp.broadcast_to(cells[:, None, :], (ROWS, COLS, C)).reshape(T, C)

    place = iota((T, C), 0) & (COLS - 1)
    left = jnp.where(place == 0, rim_rows(0, col > 0), pltpu.roll(fresh, 1, 0))
    right = jnp.where(place == COLS - 1, rim_rows(1, col < STRIPS - 1), pltpu.roll(fresh, T - 1, 0))
    shifted = [left.astype(BF16), fresh.astype(BF16), right.astype(BF16)]

    a_last(2)
    spread_on(0, 2)
    spread_on(2, 0)

    for block in range(4):
        lanes = iota((1, 512), 1)
        within = lanes & 31
        channel = 32 * block + SHARD * (lanes >> 5) + within
        cells = slice(128 * block, 128 * block + 256)
        part = None
        for tap in range(3):
            inside = (within >= SHARD * tap) & (within < SHARD * (tap + 1))
            wanted = jnp.where(inside, channel - SHARD * tap, -1)
            chosen = jnp.where(iota((256, 512), 0) == wanted, 1.0, 0.0).astype(BF16)
            term = jnp.dot(shifted[tap][:, cells], chosen, preferred_element_type=F32)
            part = term if part is None else part + term
        packed[block] = part.astype(BF16)
        if block == 0:
            spread_on(3, 3)
            spread_on(3, 1)
            spread_on(1, 3)
            spread_on(1, 1)
        if block == 1:
            spread_on(3, 2)
            spread_on(1, 2)
        if block == 2:
            spread_on(2, 3)
            spread_on(2, 1)
    finish(0)
    spread_on(2, 2)

    take = iota((240, 256), 0)
    lanes = iota((240, 256), 1)
    tap_of = jnp.where(take >= 160, 2, jnp.where(take >= 80, 1, 0))
    channel = take - 80 * tap_of
    place = (lanes & 31) - SHARD * tap_of
    pick = (place >= 0) & (place < SHARD) & (channel == SHARD * (lanes >> 5) + place)
    pick = jnp.where(pick, 1.0, 0.0).astype(BF16)


    conv_acc[...] = jnp.zeros_like(conv_acc)

    def multiply(dq):
        block = ring(zl + dq, 4)
        landed(whole(dq, 1 - core), arr_ws.at[dq])
        cells = packed[block]
        for tap in range(3):
            weights = wg[tap, pl.ds(block * 16, 16)].reshape(512, C)
            conv_acc[tap] += jnp.dot(cells, weights, preferred_element_type=F32)
        for part in range(2):
            rows = wg[3, pl.ds(block * 16 + part * 8, 8)].reshape(256, C)
            rows = jnp.dot(pick, rows, preferred_element_type=F32).astype(BF16)
            start = pl.multiple_of(block * 160 + part * 80, 80)
            for tap in range(3):
                wq[tap, pl.ds(start, 80)] = rows[80 * tap : 80 * (tap + 1)]

    def arrived(which, dz):
        landed(kvp.at[which, place_of(dz)], arr_p.at[which, dz])

    def share(dz):
        strip = kvp.at[:, place_of(dz)]
        send(strip, strip, arr_ps.at[dz], sibling)

    arrived(0, 3)
    send(kvp.at[0, place_of(3)], kvp.at[1, place_of(3)], arr_p.at[1, 2], at_zh(1))
    arrived(1, 1)
    send(kvp.at[1, place_of(1)], kvp.at[0, place_of(1)], arr_p.at[0, 2], at_zh(-1))
    send(kv_ref.at[0, :, last], kv4.at[col, 0], arr_4.at[3, 0], at_zh(1))
    send(kv_ref.at[1, :, last], kv4.at[col, 1], arr_4.at[1, 1], at_zh(-1))
    finish(3)
    multiply(0)
    finish(1)
    multiply(3)
    finish(2)
    multiply(1)
    multiply(2)

    blank = jnp.zeros((COLS, C), F32)
    above = jnp.concatenate([blank, conv_acc[0, : T - COLS]], axis=0)
    below = jnp.concatenate([conv_acc[2, COLS:], blank], axis=0)
    latent = lat_ref[...].astype(F32).reshape(T, C)
    block_out = (latent + (above + conv_acc[1] + below) + bias_ref[...].reshape(1, C)).astype(BF16)
    block_ref[...] = block_out.astype(F32).reshape(ROWS, COLS, C).astype(BF16)
    cells = block_out.astype(F32)
    centered = cells - jnp.mean(cells, axis=1, keepdims=True)
    variance = jnp.mean(centered * centered, axis=1, keepdims=True)
    cells = (centered * lax.rsqrt(variance + EPS) * again_ref[...].reshape(1, C).reshape(1, C)).astype(BF16)

    queries = jnp.dot(cells, wq[0], preferred_element_type=F32).astype(BF16)
    for pair in range(PAIRS):
        qs[pair] = queries[:, pair * 128 : (pair + 1) * 128]
    send(qs.at[ring(zh + 1, 4)], qin.at[0], arr_q.at[0], at_zh(1))
    send(qs.at[ring(zh + 2, 4)], qin.at[1], arr_q.at[1], at_zh(-1))
    send(kv_ref.at[1, :, last], kv4.at[col, 1], arr_4.at[3, 1], at_zh(1))
    send(kv_ref.at[0, :, last], kv4.at[col, 0], arr_4.at[1, 0], at_zh(-1))
    qin[2] = qs[zh]
    qin[3] = qs[ring(zh - 1, 4)]
    for tap in (1, 2):
        projected = jnp.dot(cells, wq[tap], preferred_element_type=F32).astype(BF16)
        fkv_ref[tap - 1] = projected.astype(F32).reshape(ROWS, COLS, C).astype(BF16)
        kf[tap - 1] = projected

    landed(kv4.at[place_of(3), 0], arr_4.at[3, 0])
    send(kv4.at[place_of(3), 0], kv4.at[place_of(3), 0], arr_4.at[2, 0], at_zh(1))
    landed(kv4.at[place_of(1), 1], arr_4.at[1, 1])
    send(kv4.at[place_of(1), 1], kv4.at[place_of(1), 1], arr_4.at[2, 1], at_zh(-1))
    for dz in (3, 1):
        arrived(dz // 3, dz)
        share(dz)
    for keep in kept:
        keep.wait()

    @pl.loop(0, PAIRS - 1)
    def _(pair):
        lanes = lanes_of(pair)
        result, level = part_of(qs[pair], [(lambda: kf[0, :, lanes], lambda: kf[1, :, lanes])])
        fresh_o[pair] = result
        fresh_l[pair] = level

    for which in range(2):
        arrived(which, 2)
    share(2)
    landed(kvp.at[0, place_of(0, False)], arr_ps.at[0])
    landed(kvp.at[1, place_of(0, False)], arr_ps.at[4])
    for dz in (3, 1, 2):
        landed(kvp.at[:, place_of(dz, False)], arr_ps.at[dz])

    def strips_but(mine, ref):
        def block(step, kv):
            return lambda: ref[lax.rem(mine + 1 + step, STRIPS), kv]

        return [(block(step, 0), block(step, 1)) for step in range(STRIPS - 1)]

    def give(turn):
        home, pair = at_zh(3 - 2 * turn), ring(zh - turn, 4)
        results = copy(rout.at[turn], rin.at[pair], arr_r.at[turn], home, 120 + turn)
        levels = copy(sout.at[turn], sin.at[pair], arr_s.at[turn], home, 124 + turn)
        return results, levels

    @pl.loop(0, 4)
    def _(turn):
        remote = turn < 2
        which = lax.rem(turn, 2)
        source = ring(zh + jnp.where(remote, 3 - 2 * turn, 0), 4)

        @pl.when(remote)
        def _():
            landed(qin.at[turn], arr_q.at[turn])

        result, level = part_of(qin[turn], strips_but(source * 2 + core, kvp.at[which]))
        level = level.T
        level = jnp.where(iota((8, T), 0) == 0, level[0:1], level[HEAD_DIM : HEAD_DIM + 1])

        @pl.when(remote)
        def _():
            rout[turn] = result.astype(BF16)
            sout[turn] = level
            for outgoing in give(turn):
                outgoing.start()

        @pl.when(turn >= 2)
        def _():
            pair = ring(zh + 2 - turn, 4)
            rin[pair] = result.astype(BF16)
            sin[pair] = level

    def put(pair, result):
        att_ref[:, :, pair * 128 : (pair + 1) * 128] = result.reshape(ROWS, COLS, 128).astype(BF16)

    furthest = kv4.at[place_of(2)]
    landed(kv4.at[place_of(3), 1], arr_4.at[3, 1])
    landed(kv4.at[place_of(1), 0], arr_4.at[1, 0])
    for dz in (3, 1):
        send(kv4.at[place_of(dz)], kv4.at[place_of(dz)], arr_4s.at[dz], sibling)

    def strips_at(places):
        def block(place, kv):
            return lambda: kv4[place, kv]

        return [(block(place, 0), block(place, 1)) for place in places]

    for dz in (0, 3, 1):
        landed(kv4.at[place_of(dz, False)], arr_4s.at[dz])
    near = [(lambda: kf[0, :, last], lambda: kf[1, :, last])]
    near += strips_at([place_of(0, False)] + [place_of(dz, mine) for dz in (3, 1) for mine in (True, False)])
    near_o, near_l = part_of(qs[PAIRS - 1], near)
    for kv in range(2):
        landed(kv4.at[place_of(2), kv], arr_4.at[2, kv])
    furthest = kv4.at[place_of(2)]
    send(furthest, furthest, arr_4s.at[2], sibling)
    landed(kv4.at[place_of(2, False)], arr_4s.at[2])
    far_o, far_l = part_of(qs[PAIRS - 1], strips_at([place_of(2), place_of(2, False)]))

    def merged(result, level, other, other_level):
        most = jnp.maximum(level, other_level)
        old, new = jnp.exp2(level - most), jnp.exp2(other_level - most)
        return (result * old + other * new) / (old + new)

    put(PAIRS - 1, merged(near_o, near_l, far_o, far_l))

    for turn in range(2):
        pair = ring(zh + 1 + turn, 4)
        landed(rin.at[pair], arr_r.at[turn])
        landed(sin.at[pair], arr_s.at[turn])
    for pair in range(PAIRS - 1):
        level = jnp.where(iota((128, T), 0) < HEAD_DIM, sin[pair, 0:1], sin[pair, 1:2]).T
        put(pair, merged(rin[pair].astype(F32), level, fresh_o[pair], fresh_l[pair]))

    for turn in range(2):
        for outgoing in give(turn):
            outgoing.wait_send()
    for started in sent:
        started.wait_send()


def on_device(
    latent, stale_rim, stale_kv, norm_gain, norm_shift, conv_weight, conv_bias, attn_gain, qkv_weight
):
    taps = conv_weight.reshape(3, 3 * SHARD, C)
    projections = qkv_weight.reshape(SHARD, 3, C).transpose(1, 0, 2).reshape(1, 3 * SHARD, C)
    weights = jnp.concatenate([taps, projections], axis=0)
    weights = jnp.pad(weights, ((0, 0), (0, 2), (0, 0)))
    vmem = pl.BlockSpec(memory_space=pltpu.VMEM)
    dma = pltpu.SemaphoreType.DMA
    cells = jax.ShapeDtypeStruct((ROWS, COLS, C), BF16)
    block, attended, fresh_kv = pl.pallas_call(
        kernel,
        out_shape=(cells, cells, jax.ShapeDtypeStruct((2, ROWS, COLS, C), BF16)),
        in_specs=[vmem, vmem, pl.BlockSpec(memory_space=pl.ANY)] + [vmem] * 5,
        out_specs=(vmem, vmem, vmem),
        scratch_shapes=[
            pltpu.VMEM((4, SHARDS, 32, C), BF16),
            pltpu.VMEM((2, STRIPS, 2, T, 128), BF16),
            pltpu.VMEM((STRIPS, 2, T, 128), BF16),
            pltpu.VMEM((STRIPS, 8, 128), F32),
            pltpu.VMEM((2, ROWS, C), BF16),
            pltpu.VMEM((2, ROWS, C), BF16),
            pltpu.VMEM((4, T, 512), BF16),
            pltpu.VMEM((3, T, C), F32),
            pltpu.VMEM((3, C, C), BF16),
            pltpu.VMEM((PAIRS, T, 128), BF16),
            pltpu.VMEM((4, T, 128), BF16),
            pltpu.VMEM((2, T, C), BF16),
            pltpu.VMEM((4, T, 128), F32),
            pltpu.VMEM((4, T, 128), F32),
            pltpu.VMEM((2, T, 128), BF16),
            pltpu.VMEM((2, 8, T), F32),
            pltpu.VMEM((4, T, 128), BF16),
            pltpu.VMEM((4, 8, T), F32),
            dma((128,)),
            dma((2,)),
            dma((3,)),
            dma((4, 3)),
            dma((4, 4, 3)),
            dma((4,)),
            dma((STRIPS,)),
            dma((2,)),
            dma((2, 4)),
            dma((4, 2)),
            dma((5,)),
            dma((4,)),
            dma((2,)),
            dma((2,)),
            dma((2,)),
        ],
        compiler_params=pltpu.CompilerParams(
            collective_id=0, has_side_effects=True, vmem_limit_bytes=56 * 2**20
        ),
    )(
        latent.reshape(ROWS, COLS, C),
        stale_rim.reshape(ROWS, COLS, C),
        stale_kv.reshape(2, T, C),
        norm_gain,
        norm_shift,
        weights,
        conv_bias,
        attn_gain,
    )
    shape = latent.shape
    return block.reshape(shape), attended.reshape(shape), fresh_kv.reshape((2,) + shape)


def solution(mesh):
    cells = P("row", None, "col", None)
    pairs = P(None, "row", None, "col", None)
    return jax.shard_map(
        on_device,
        mesh=mesh,
        in_specs=(cells, cells, pairs, P(), P(), P(None, "row", None), P(), P(), P("row", None)),
        out_specs=(cells, cells, pairs),
        check_vma=False,
    )
```

```python
import jax
import jax.numpy as jnp
from jax import lax
from jax.experimental import pallas as pl
from jax.experimental.pallas import tpu as pltpu
from jax.sharding import PartitionSpec as P

HEADS = 10
HEAD_DIM = 64
GROUPS = 16
C = 640
ROWS = 32
COLS = 8
T = ROWS * COLS
STRIPS = 8
SHARD = 10
SHARDS = 64
PAIRS = 5
EPS = 1e-05
LOG2E = 1.4426950408889634
MESH = pl.DeviceIdType.MESH
F32 = jnp.float32
BF16 = jnp.bfloat16


def iota(shape, dim):
    return lax.broadcasted_iota(jnp.int32, shape, dim)


def part_of(q, blocks):
    low = iota((T, 128), 1) < HEAD_DIM
    scaled = q.astype(F32) * HEAD_DIM ** -0.5
    found = []
    for head in range(2):
        mine = jnp.where(low, scaled, 0.0) if head == 0 else jnp.where(low, 0.0, scaled)
        mine = mine.astype(BF16)
        scores = [
            lax.dot_general(mine, keys(), (((1,), (1,)), ((), ())), preferred_element_type=F32)
            for keys, _ in blocks
        ]
        best = scores[0]
        for score in scores[1:]:
            best = jnp.maximum(best, score)
        top = jnp.max(best, axis=1, keepdims=True) * LOG2E
        total = result = None
        for score, (_, values) in zip(scores, blocks):
            weights = jnp.exp2(score * LOG2E - top)
            term = jnp.dot(weights.astype(BF16), values(), preferred_element_type=F32)
            total = weights if total is None else total + weights
            result = term if result is None else result + term
        total = jnp.sum(total, axis=1, keepdims=True)
        found.append((result / total, top + jnp.log(total) * LOG2E))
    result = jnp.where(low, found[0][0], found[1][0])
    return result, jnp.where(low, found[0][1], found[1][1])


def kernel(
    lat_ref, rim_ref, kv_ref, gain_ref, shift_ref, w_ref, bias_ref, again_ref,
    block_ref, att_ref, fkv_ref,
    wg, kvp, kv4, stats, edges, halo, packed, conv_acc, wq,
    qs, qin, kf, fresh_o, fresh_l, rout, sout, rin, sin,
    sems, own_sem, arr_wz, arr_wa, arr_wb, arr_ws, arr_st, arr_h,
    arr_p, arr_4, arr_ps, arr_4s, arr_q, arr_r, arr_s,
):
    row, col = lax.axis_index("row"), lax.axis_index("col")
    zl, xy = lax.div(row, 16), lax.rem(row, 16)
    x, y = lax.div(xy, 4), lax.rem(xy, 4)
    zh, core = lax.div(col, 2), lax.rem(col, 2)
    a, b = x + core * (y - x), y + core * (x - y)
    sa, sb = 4 - 3 * core, 1 + 3 * core

    def ring(value, size):
        return lax.rem(value + size, size)

    def at_a(step):
        return (zl * 16 + ring(a + step, 4) * sa + b * sb, col)

    def at_b(step):
        return (zl * 16 + a * sa + ring(b + step, 4) * sb, col)

    def at_z(step):
        z = ring(zh * 4 + zl + step, 16)
        return (lax.rem(z, 4) * 16 + xy, lax.div(z, 4) * 2 + core)

    def at_zh(step):
        return (row, ring(zh + step, 4) * 2 + core)

    def at_col(step):
        return (row, ring(col + step, 8))

    sibling = (row, col + 1 - 2 * core)

    barrier = pltpu.get_barrier_semaphore()
    partners = [at_a(1), at_a(-1), at_a(2), at_b(1), at_b(-1), at_z(1), at_z(-1), at_z(4 * core - 2)]
    partners += [at_col(step) for step in range(1, STRIPS)]
    for partner in partners:
        pl.semaphore_signal(barrier, inc=1, device_id=partner, device_id_type=MESH)

    sent = []

    def copy(src, dst, arrived, device, index=None):
        index = len(sent) if index is None else index
        return pltpu.make_async_remote_copy(
            src_ref=src, dst_ref=dst, send_sem=sems.at[index], recv_sem=arrived,
            device_id=device, device_id_type=MESH,
        )

    def send(src, dst, arrived, device):
        started = copy(src, dst, arrived, device)
        started.start()
        sent.append(started)

    def landed(dst, arrived):
        copy(dst, dst, arrived, sibling, 0).wait_recv()

    half = pl.ds(2 * core, 2)

    def lanes_of(pair):
        return pl.ds(pl.multiple_of(pair * 128, 128), 128)

    wg[half, pl.ds(row, 1)] = w_ref[half][:, None]
    rim = rim_ref[...].astype(F32)
    edges[0] = rim[:, 0, :].astype(BF16)
    edges[1] = rim[:, COLS - 1, :].astype(BF16)
    latent = lat_ref[...].astype(F32).reshape(T, C)
    first = jnp.sum(latent, axis=0, keepdims=True)
    second = jnp.sum(latent * latent, axis=0, keepdims=True)
    spot = iota((8, C), 0)
    member = iota((C, 128), 0) - 40 * iota((C, 128), 1)
    member = jnp.where((member >= 0) & (member < 40), 1.0, 0.0)
    exact = lax.Precision.HIGHEST
    stats[col] = jnp.dot(
        jnp.where(spot == 0, first, jnp.where(spot == 1, second, 0.0)), member,
        precision=exact, preferred_element_type=F32,
    )

    kept = [
        pltpu.make_async_copy(kv_ref.at[:, :, lanes_of(ring(zh - which, 4))], kvp.at[which, col], own_sem.at[which])
        for which in range(2)
    ]
    for keep in kept:
        keep.start()

    pl.semaphore_wait(barrier, len(partners))

    def shard(q, ia, ib):
        return wg.at[half, ring(q, 4) * 16 + ring(ia, 4) * sa + ring(ib, 4) * sb]

    def z_send(step, slot):
        piece = shard(zl, a, b)
        send(piece, piece, arr_wz.at[slot], at_z(step))

    def z_landed(dq, slot):
        landed(shard(zl + dq, a, b), arr_wz.at[slot])

    def b_send(dq, da, db, step, slot):
        piece = shard(zl + dq, a + da, b + db)
        send(piece, piece, arr_wb.at[dq, da, slot], at_b(step))

    def b_landed(dq, da, db, slot):
        landed(shard(zl + dq, a + da, b + db), arr_wb.at[dq, da, slot])

    def spread(dq, da):
        b_send(dq, da, 0, 1, 0)
        b_send(dq, da, 0, -1, 1)

    def spread_on(dq, da):
        b_landed(dq, da, -1, 0)
        b_landed(dq, da, 1, 1)
        if (dq + da) % 2:
            b_send(dq, da, 1, -1, 2)
        else:
            b_send(dq, da, -1, 1, 2)

    def a_start(dq):
        piece = shard(zl + dq, a, b)
        for slot, step in ((0, 1), (1, -1), (2, 2)):
            send(piece, piece, arr_wa.at[dq, slot], at_a(step))
        spread(dq, 0)

    def a_next(dq):
        for slot, da in ((0, 3), (1, 1)):
            landed(shard(zl + dq, a + da, b), arr_wa.at[dq, slot])
            spread(dq, da)

    def a_last(dq):
        landed(shard(zl + dq, a + 2, b), arr_wa.at[dq, 2])
        spread(dq, 2)

    def whole(dq, which):
        return wg.at[pl.ds(2 * which, 2), pl.ds(ring(zl + dq, 4) * 16, 16)]

    def finish(dq):
        for da in range(4):
            b_landed(dq, da, 2, 2)
        send(whole(dq, core), whole(dq, core), arr_ws.at[dq], sibling)

    def place_of(dz, mine=True):
        return ring(zh + dz, 4) * 2 + (core if mine else 1 - core)

    for step in range(1, STRIPS):
        send(stats.at[col], stats.at[col], arr_st.at[step], at_col(step))
    z_send(1, 0)
    z_send(-1, 1)
    z_send(2 - 4 * core, 2)
    a_start(0)
    send(edges.at[1], halo.at[0], arr_h.at[0], at_col(1))
    send(edges.at[0], halo.at[1], arr_h.at[1], at_col(-1))

    def pair_of(dz):
        return kv_ref.at[:, :, lanes_of(ring(zh + dz, 4))]

    send(pair_of(1), kvp.at[0, col], arr_p.at[0, 3], at_zh(1))
    send(pair_of(-2), kvp.at[1, col], arr_p.at[1, 1], at_zh(-1))
    send(pair_of(0), kvp.at[1, col], arr_p.at[1, 3], at_zh(1))
    send(pair_of(-1), kvp.at[0, col], arr_p.at[0, 1], at_zh(-1))
    last = lanes_of(PAIRS - 1)
    send(kv_ref.at[0, :, last], kv4.at[col, 0], arr_4.at[3, 0], at_zh(1))
    send(kv_ref.at[1, :, last], kv4.at[col, 1], arr_4.at[1, 1], at_zh(-1))
    send(pair_of(0), kvp.at[0, col], arr_ps.at[0], sibling)
    send(pair_of(-1), kvp.at[1, col], arr_ps.at[4], sibling)
    send(kv_ref.at[:, :, last], kv4.at[col], arr_4s.at[0], sibling)

    a_next(0)
    z_landed(3, 0)
    a_start(3)
    z_landed(1, 1)
    a_start(1)
    a_last(0)
    z_landed(2, 2)
    a_start(2)
    spread_on(0, 0)

    a_next(3)
    a_next(1)
    spread_on(0, 3)
    spread_on(0, 1)
    for step in range(1, STRIPS):
        landed(stats.at[ring(col - step, STRIPS)], arr_st.at[step])
    sums = stats[0]
    for strip in range(1, STRIPS):
        sums = sums + stats[strip]
    back = iota((128, C), 1) - 40 * iota((128, C), 0)
    back = jnp.where((back >= 0) & (back < 40), 1.0, 0.0)
    grouped = jnp.dot(sums, back, precision=exact, preferred_element_type=F32)
    count = T * STRIPS * (C // GROUPS)
    average = grouped[0:1] / count
    spread_of = grouped[1:2] / count - average * average
    factor = lax.rsqrt(spread_of + EPS)


    latent = lat_ref[...].astype(F32).reshape(T, C)
    normed = (latent - average) * factor * gain_ref[...].reshape(1, C) + shift_ref[...].reshape(1, C)
    fresh = (normed / (1.0 + jnp.exp(-normed))).astype(BF16).astype(F32)

    a_last(3)
    a_last(1)
    a_next(2)
    spread_on(3, 0)
    spread_on(1, 0)

    landed(halo.at[0], arr_h.at[0])
    landed(halo.at[1], arr_h.at[1])

    def rim_rows(side, present):
        cells = jnp.where(present, halo[side].astype(F32), 0.0)
        return jnp.broadcast_to(cells[:, None, :], (ROWS, COLS, C)).reshape(T, C)

    place = iota((T, C), 0) & (COLS - 1)
    left = jnp.where(place == 0, rim_rows(0, col > 0), pltpu.roll(fresh, 1, 0))
    right = jnp.where(place == COLS - 1, rim_rows(1, col < STRIPS - 1), pltpu.roll(fresh, T - 1, 0))
    shifted = [left.astype(BF16), fresh.astype(BF16), right.astype(BF16)]

    a_last(2)
    spread_on(0, 2)
    spread_on(2, 0)

    for block in range(4):
        lanes = iota((1, 512), 1)
        within = lanes & 31
        channel = 32 * block + SHARD * (lanes >> 5) + within
        cells = slice(128 * block, 128 * block + 256)
        part = None
        for tap in range(3):
            inside = (within >= SHARD * tap) & (within < SHARD * (tap + 1))
            wanted = jnp.where(inside, channel - SHARD * tap, -1)
            chosen = jnp.where(iota((256, 512), 0) == wanted, 1.0, 0.0).astype(BF16)
            term = jnp.dot(shifted[tap][:, cells], chosen, preferred_element_type=F32)
            part = term if part is None else part + term
        packed[block] = part.astype(BF16)
        if block == 0:
            spread_on(3, 3)
            spread_on(3, 1)
            spread_on(1, 3)
            spread_on(1, 1)
        if block == 1:
            spread_on(3, 2)
            spread_on(1, 2)
        if block == 2:
            spread_on(2, 3)
            spread_on(2, 1)
    finish(0)
    spread_on(2, 2)

    take = iota((240, 256), 0)
    lanes = iota((240, 256), 1)
    tap_of = jnp.where(take >= 160, 2, jnp.where(take >= 80, 1, 0))
    channel = take - 80 * tap_of
    place = (lanes & 31) - SHARD * tap_of
    pick = (place >= 0) & (place < SHARD) & (channel == SHARD * (lanes >> 5) + place)
    pick = jnp.where(pick, 1.0, 0.0).astype(BF16)


    conv_acc[...] = jnp.zeros_like(conv_acc)

    def multiply(dq):
        block = ring(zl + dq, 4)
        landed(whole(dq, 1 - core), arr_ws.at[dq])
        cells = packed[block]
        for tap in range(3):
            weights = wg[tap, pl.ds(block * 16, 16)].reshape(512, C)
            conv_acc[tap] += jnp.dot(cells, weights, preferred_element_type=F32)
        for part in range(2):
            rows = wg[3, pl.ds(block * 16 + part * 8, 8)].reshape(256, C)
            rows = jnp.dot(pick, rows, preferred_element_type=F32).astype(BF16)
            start = pl.multiple_of(block * 160 + part * 80, 80)
            for tap in range(3):
                wq[tap, pl.ds(start, 80)] = rows[80 * tap : 80 * (tap + 1)]

    def arrived(which, dz):
        landed(kvp.at[which, place_of(dz)], arr_p.at[which, dz])

    def share(dz):
        strip = kvp.at[:, place_of(dz)]
        send(strip, strip, arr_ps.at[dz], sibling)

    arrived(0, 3)
    send(kvp.at[0, place_of(3)], kvp.at[1, place_of(3)], arr_p.at[1, 2], at_zh(1))
    arrived(1, 1)
    send(kvp.at[1, place_of(1)], kvp.at[0, place_of(1)], arr_p.at[0, 2], at_zh(-1))
    finish(3)
    multiply(0)
    finish(1)
    multiply(3)
    finish(2)
    multiply(1)
    multiply(2)

    blank = jnp.zeros((COLS, C), F32)
    above = jnp.concatenate([blank, conv_acc[0, : T - COLS]], axis=0)
    below = jnp.concatenate([conv_acc[2, COLS:], blank], axis=0)
    latent = lat_ref[...].astype(F32).reshape(T, C)
    block_out = (latent + (above + conv_acc[1] + below) + bias_ref[...].reshape(1, C)).astype(BF16)
    block_ref[...] = block_out.astype(F32).reshape(ROWS, COLS, C).astype(BF16)
    cells = block_out.astype(F32)
    centered = cells - jnp.mean(cells, axis=1, keepdims=True)
    variance = jnp.mean(centered * centered, axis=1, keepdims=True)
    cells = (centered * lax.rsqrt(variance + EPS) * again_ref[...].reshape(1, C).reshape(1, C)).astype(BF16)

    queries = jnp.dot(cells, wq[0], preferred_element_type=F32).astype(BF16)
    for pair in range(PAIRS):
        qs[pair] = queries[:, pair * 128 : (pair + 1) * 128]
    send(qs.at[ring(zh + 1, 4)], qin.at[0], arr_q.at[0], at_zh(1))
    send(qs.at[ring(zh + 2, 4)], qin.at[1], arr_q.at[1], at_zh(-1))
    send(kv_ref.at[1, :, last], kv4.at[col, 1], arr_4.at[3, 1], at_zh(1))
    send(kv_ref.at[0, :, last], kv4.at[col, 0], arr_4.at[1, 0], at_zh(-1))
    qin[2] = qs[zh]
    qin[3] = qs[ring(zh - 1, 4)]
    for tap in (1, 2):
        projected = jnp.dot(cells, wq[tap], preferred_element_type=F32).astype(BF16)
        fkv_ref[tap - 1] = projected.astype(F32).reshape(ROWS, COLS, C).astype(BF16)
        kf[tap - 1] = projected

    landed(kv4.at[place_of(3), 0], arr_4.at[3, 0])
    send(kv4.at[place_of(3), 0], kv4.at[place_of(3), 0], arr_4.at[2, 0], at_zh(1))
    landed(kv4.at[place_of(1), 1], arr_4.at[1, 1])
    send(kv4.at[place_of(1), 1], kv4.at[place_of(1), 1], arr_4.at[2, 1], at_zh(-1))
    for dz in (3, 1):
        arrived(dz // 3, dz)
        share(dz)
    for keep in kept:
        keep.wait()

    @pl.loop(0, PAIRS - 1)
    def _(pair):
        lanes = lanes_of(pair)
        result, level = part_of(qs[pair], [(lambda: kf[0, :, lanes], lambda: kf[1, :, lanes])])
        fresh_o[pair] = result
        fresh_l[pair] = level

    for which in range(2):
        arrived(which, 2)
    share(2)
    landed(kvp.at[0, place_of(0, False)], arr_ps.at[0])
    landed(kvp.at[1, place_of(0, False)], arr_ps.at[4])
    for dz in (3, 1, 2):
        landed(kvp.at[:, place_of(dz, False)], arr_ps.at[dz])

    def strips_but(mine, ref):
        def block(step, kv):
            return lambda: ref[lax.rem(mine + 1 + step, STRIPS), kv]

        return [(block(step, 0), block(step, 1)) for step in range(STRIPS - 1)]

    def give(turn):
        home, pair = at_zh(3 - 2 * turn), ring(zh - turn, 4)
        results = copy(rout.at[turn], rin.at[pair], arr_r.at[turn], home, 120 + turn)
        levels = copy(sout.at[turn], sin.at[pair], arr_s.at[turn], home, 124 + turn)
        return results, levels

    @pl.loop(0, 4)
    def _(turn):
        remote = turn < 2
        which = lax.rem(turn, 2)
        source = ring(zh + jnp.where(remote, 3 - 2 * turn, 0), 4)

        @pl.when(remote)
        def _():
            landed(qin.at[turn], arr_q.at[turn])

        result, level = part_of(qin[turn], strips_but(source * 2 + core, kvp.at[which]))
        level = level.T
        level = jnp.where(iota((8, T), 0) == 0, level[0:1], level[HEAD_DIM : HEAD_DIM + 1])

        @pl.when(remote)
        def _():
            rout[turn] = result.astype(BF16)
            sout[turn] = level
            for outgoing in give(turn):
                outgoing.start()

        @pl.when(turn >= 2)
        def _():
            pair = ring(zh + 2 - turn, 4)
            rin[pair] = result.astype(BF16)
            sin[pair] = level

    def put(pair, result):
        att_ref[:, :, pair * 128 : (pair + 1) * 128] = result.reshape(ROWS, COLS, 128).astype(BF16)

    furthest = kv4.at[place_of(2)]
    landed(kv4.at[place_of(3), 1], arr_4.at[3, 1])
    landed(kv4.at[place_of(1), 0], arr_4.at[1, 0])
    for dz in (3, 1):
        send(kv4.at[place_of(dz)], kv4.at[place_of(dz)], arr_4s.at[dz], sibling)

    def strips_at(places):
        def block(place, kv):
            return lambda: kv4[place, kv]

        return [(block(place, 0), block(place, 1)) for place in places]

    for dz in (0, 3, 1):
        landed(kv4.at[place_of(dz, False)], arr_4s.at[dz])
    near = [(lambda: kf[0, :, last], lambda: kf[1, :, last])]
    near += strips_at([place_of(0, False)] + [place_of(dz, mine) for dz in (3, 1) for mine in (True, False)])
    near_o, near_l = part_of(qs[PAIRS - 1], near)
    for kv in range(2):
        landed(kv4.at[place_of(2), kv], arr_4.at[2, kv])
    furthest = kv4.at[place_of(2)]
    send(furthest, furthest, arr_4s.at[2], sibling)
    landed(kv4.at[place_of(2, False)], arr_4s.at[2])
    far_o, far_l = part_of(qs[PAIRS - 1], strips_at([place_of(2), place_of(2, False)]))

    def merged(result, level, other, other_level):
        most = jnp.maximum(level, other_level)
        old, new = jnp.exp2(level - most), jnp.exp2(other_level - most)
        return (result * old + other * new) / (old + new)

    put(PAIRS - 1, merged(near_o, near_l, far_o, far_l))

    for turn in range(2):
        pair = ring(zh + 1 + turn, 4)
        landed(rin.at[pair], arr_r.at[turn])
        landed(sin.at[pair], arr_s.at[turn])
    for pair in range(PAIRS - 1):
        level = jnp.where(iota((128, T), 0) < HEAD_DIM, sin[pair, 0:1], sin[pair, 1:2]).T
        put(pair, merged(rin[pair].astype(F32), level, fresh_o[pair], fresh_l[pair]))

    for turn in range(2):
        for outgoing in give(turn):
            outgoing.wait_send()
    for started in sent:
        started.wait_send()


def on_device(
    latent, stale_rim, stale_kv, norm_gain, norm_shift, conv_weight, conv_bias, attn_gain, qkv_weight
):
    taps = conv_weight.reshape(3, 3 * SHARD, C)
    projections = qkv_weight.reshape(SHARD, 3, C).transpose(1, 0, 2).reshape(1, 3 * SHARD, C)
    weights = jnp.concatenate([taps, projections], axis=0)
    weights = jnp.pad(weights, ((0, 0), (0, 2), (0, 0)))
    vmem = pl.BlockSpec(memory_space=pltpu.VMEM)
    dma = pltpu.SemaphoreType.DMA
    cells = jax.ShapeDtypeStruct((ROWS, COLS, C), BF16)
    block, attended, fresh_kv = pl.pallas_call(
        kernel,
        out_shape=(cells, cells, jax.ShapeDtypeStruct((2, ROWS, COLS, C), BF16)),
        in_specs=[vmem, vmem, pl.BlockSpec(memory_space=pl.ANY)] + [vmem] * 5,
        out_specs=(vmem, vmem, vmem),
        scratch_shapes=[
            pltpu.VMEM((4, SHARDS, 32, C), BF16),
            pltpu.VMEM((2, STRIPS, 2, T, 128), BF16),
            pltpu.VMEM((STRIPS, 2, T, 128), BF16),
            pltpu.VMEM((STRIPS, 8, 128), F32),
            pltpu.VMEM((2, ROWS, C), BF16),
            pltpu.VMEM((2, ROWS, C), BF16),
            pltpu.VMEM((4, T, 512), BF16),
            pltpu.VMEM((3, T, C), F32),
            pltpu.VMEM((3, C, C), BF16),
            pltpu.VMEM((PAIRS, T, 128), BF16),
            pltpu.VMEM((4, T, 128), BF16),
            pltpu.VMEM((2, T, C), BF16),
            pltpu.VMEM((4, T, 128), F32),
            pltpu.VMEM((4, T, 128), F32),
            pltpu.VMEM((2, T, 128), BF16),
            pltpu.VMEM((2, 8, T), F32),
            pltpu.VMEM((4, T, 128), BF16),
            pltpu.VMEM((4, 8, T), F32),
            dma((128,)),
            dma((2,)),
            dma((3,)),
            dma((4, 3)),
            dma((4, 4, 3)),
            dma((4,)),
            dma((STRIPS,)),
            dma((2,)),
            dma((2, 4)),
            dma((4, 2)),
            dma((5,)),
            dma((4,)),
            dma((2,)),
            dma((2,)),
            dma((2,)),
        ],
        compiler_params=pltpu.CompilerParams(
            collective_id=0, has_side_effects=True, vmem_limit_bytes=56 * 2**20
        ),
    )(
        latent.reshape(ROWS, COLS, C),
        stale_rim.reshape(ROWS, COLS, C),
        stale_kv.reshape(2, T, C),
        norm_gain,
        norm_shift,
        weights,
        conv_bias,
        attn_gain,
    )
    shape = latent.shape
    return block.reshape(shape), attended.reshape(shape), fresh_kv.reshape((2,) + shape)


def solution(mesh):
    cells = P("row", None, "col", None)
    pairs = P(None, "row", None, "col", None)
    return jax.shard_map(
        on_device,
        mesh=mesh,
        in_specs=(cells, cells, pairs, P(), P(), P(None, "row", None), P(), P(), P("row", None)),
        out_specs=(cells, cells, pairs),
        check_vma=False,
    )
```
